32 devices in a mesh: dp: 4 (over y, core), expert: 8 (over z, x).
Axes of the slice: x: 2, y: 2, z: 4, core: 2. Of those that a mesh axis runs over, the one named last changes fastest.
Arguments:
- tokens: bfloat16 [512, 7168], P('expert', 'dp'), may hold values from -6 to 6
- expert_ids: int32 [512, 8], P('expert'), may hold values from 0 to 63, all different within a row; in each aligned block of 64 rows (0 to 63, 64 to 127, ...) at most 10 rows name the same one
- combine_weights: float32 [512, 8], P('expert'), may hold values from 0.05 to 0.6
- w_gate: bfloat16 [64, 7168, 1024], P('expert', 'dp'), may hold values from -0.0625 to 0.0625
- w_up: bfloat16 [64, 7168, 1024], P('expert', 'dp'), may hold values from -0.0625 to 0.0625
- w_down: bfloat16 [64, 1024, 7168], P('expert', None, 'dp'), may hold values from -0.1875 to 0.1875
Outputs:
- combined: bfloat16 [512, 7168], P('expert', 'dp')
The draws below stay inside these ranges and needn't reach their ends.
Inputs may be any that keep to these rules, and one draw needn't show every extreme that they name: `expert_ids`: each row names 8 different experts. Within the rows of one device (aligned blocks of 64 rows) no expert is named by more than 10 rows, a bound that some block reaches.
All inputs are finite; a program needn't handle non-finite values.
Results may differ from the reference program's by a relative error of at most 0.0057.
Values may be sent and summed in bfloat16 or wider, within the bound.
No kernel may reach another device: no remote copies, remote signals or barrier semaphores. Data moves between devices by JAX's collectives and lax.ppermute only.
A program may use at most 192 MiB of HBM per device.

```python
import math
import jax
import jax.numpy as jnp
import numpy as np
from jax import lax

D = 7168
TOP = 8
FF = 1024
EXPERTS = 64
TOK_DEV = 64
TOKENS = 512
CAP = 10
N_EXPERT = 8


def levels(stream_key, dims, pieces, smallest, largest):
    def one(dim, parts):
        draws = jax.random.uniform(jax.random.fold_in(jax.random.fold_in(stream_key, 6), dim), (parts,), jnp.float32, smallest / len(pieces), largest / len(pieces))
        return jnp.repeat(jnp.exp(draws), dims[dim] // parts).reshape((-1,) + (1,) * (len(dims) - dim - 1))

    level = one(*pieces[0])
    for cut in pieces[1:]:
        level = level * one(*cut)
    return level


def routed_block(stream_key, own, number, rows, amount, top, bound, slope):
    order = jax.random.permutation(stream_key, amount)
    crowded, common = shares(amount, rows * top, bound, slope, True), shares(amount, rows * top, bound, slope, False)
    places = jnp.arange(amount)

    def named(lengths, turn):
        used = int((lengths > 0).sum())
        fixed = max(1, used // 4)
        passed = fixed + (places - fixed + turn * (used - fixed)) % max(1, amount - fixed)
        return jnp.zeros((amount,), jnp.int32).at[order[jnp.where(places < fixed, places, passed)]].set(jnp.asarray(lengths, jnp.int32))

    lengths = jnp.where(number % 4 == 0, named(crowded, number // 4), named(common, number - number // 4 - 1))
    mixed = jax.random.permutation(jax.random.fold_in(own, 3), amount)
    donor, sink = mixed[0:amount // 2 * 2:2], mixed[1:amount // 2 * 2:2]
    room = jnp.minimum(lengths[donor] - 1, bound - lengths[sink]) // 2
    room = jnp.where((donor == order[0]) | (sink == order[0]) | (lengths[sink] == 0), 0, jnp.maximum(room, 0))
    passed = jax.random.randint(jax.random.fold_in(own, 4), (amount // 2,), 0, 1 << 20) % (room + 1)
    lengths = lengths.at[donor].add(-passed).at[sink].add(passed)
    items = jnp.searchsorted(jnp.cumsum(lengths), jnp.arange(rows * top), side="right").astype(jnp.int32)
    listing = items.reshape(top, rows).T
    listing = listing[jax.random.permutation(jax.random.fold_in(own, 1), rows)]
    turn = jax.random.randint(jax.random.fold_in(own, 2), (rows, 1), 0, top)
    return jnp.take_along_axis(listing, (jnp.arange(top)[None, :] + turn) % top, axis=1)


def shares(number_of, total, most, slope, full):
    loads = [(1 << 20) // math.isqrt(grade ** slope) + 1 for grade in range(1, number_of + 1)]
    largest = most if full else min(most, max(-(-total // number_of), total * loads[0] // sum(loads)))
    least = 1 if total - largest >= number_of - 1 else 0
    counts, spare = [largest] + [least] * (number_of - 1), total - largest - least * (number_of - 1)
    while spare > 0:
        free = [i for i in range(1, number_of) if counts[i] < largest] or [i for i in range(1, number_of) if counts[i] < most]
        whole, budget = sum([loads[i] for i in free]), spare
        for i in free:
            addition = min(most - counts[i], max(1, budget * loads[i] // whole), spare)
            counts[i] = counts[i] + addition
            spare = spare - addition
    return np.array(counts)


def normal_values(stream_key, shape, scale, most, cuts=(), held_as=jnp.bfloat16):
    entries = scale * jax.random.normal(stream_key, shape, jnp.float32)
    if cuts:
        entries = entries * levels(stream_key, shape, cuts, -0.22, 0.18)
    return jnp.clip(entries, -most, most).astype(held_as)


def setup_inputs(seed: int = 0) -> dict:
    key_of = jax.random.split(jax.random.key(seed), 7)
    tokens = normal_values(key_of[0], (TOKENS, D), 1.0, 6.0, ((0, 8), (1, 4)))
    expert_ids_keys = jax.random.split(jax.random.fold_in(key_of[1], 1), TOKENS // TOK_DEV)
    expert_ids_turns = jax.random.permutation(jax.random.fold_in(key_of[1], 3), TOKENS // TOK_DEV)
    expert_ids = jax.vmap(lambda own, number: routed_block(jax.random.fold_in(key_of[1], 2), own, number, TOK_DEV, EXPERTS, TOP, CAP, 2))(expert_ids_keys, expert_ids_turns).reshape((TOKENS, TOP))
    combine_weights = jnp.clip(jnp.exp(math.log(0.6) - 2.4849067 * jax.random.uniform(key_of[2], (TOKENS, TOP), jnp.float32) ** levels(key_of[2], (TOKENS, TOP), ((0, 8),), -0.2, 0.2)), 0.05, 0.6)
    w_gate = normal_values(key_of[3], (EXPERTS, D, FF), D ** -0.5, 0.0625, ((0, 8), (1, 4)))
    w_up = normal_values(key_of[4], (EXPERTS, D, FF), D ** -0.5, 0.0625, ((0, 8), (1, 4)))
    w_down = normal_values(key_of[5], (EXPERTS, FF, D), FF ** -0.5, 0.1875, ((0, 8), (2, 4)))
    return {"tokens": tokens, "expert_ids": expert_ids, "combine_weights": combine_weights, "w_gate": w_gate, "w_up": w_up, "w_down": w_down}


def reference(tokens, expert_ids, combine_weights, w_gate, w_up, w_down):
    limit = N_EXPERT * CAP

    def one_expert(total, item):
        number, gate_w, up_w, down_w = item
        matches = expert_ids == number
        chosen = jnp.any(matches, axis=1)
        weight_row = jnp.sum(jnp.where(matches, combine_weights, jnp.zeros_like(combine_weights)), axis=1)
        picked = jnp.nonzero(chosen, size=limit, fill_value=0)[0].astype(jnp.int32)
        valid = (jnp.arange(limit, dtype=jnp.int32) < jnp.sum(chosen.astype(jnp.int32))).astype(jnp.float32)
        arrived = tokens[picked]
        gate_sum = jnp.dot(arrived, gate_w, preferred_element_type=jnp.float32)
        up_sum = jnp.dot(arrived, up_w, preferred_element_type=jnp.float32)
        hidden = (jax.nn.silu(gate_sum) * up_sum).astype(jnp.bfloat16)
        expert_out = jnp.dot(hidden, down_w, preferred_element_type=jnp.float32).astype(jnp.bfloat16)
        scaled = (weight_row[picked] * valid)[:, None] * expert_out.astype(jnp.float32)
        return total.at[picked].add(scaled), None

    start = jnp.zeros((TOKENS, D), jnp.float32)
    numbers = jnp.arange(EXPERTS, dtype=jnp.int32)
    total, unused = lax.scan(one_expert, start, (numbers, w_gate, w_up, w_down))
    return total.astype(jnp.bfloat16)
```

```python
import functools

import jax
import jax.numpy as jnp
from jax import lax
from jax.experimental import pallas as pl
from jax.experimental.pallas import tpu as pltpu
from jax.sharding import PartitionSpec as P

CAP = 10
NEAR = 4
LANES = 128
COLUMN_PARTS = 2


def plain_shards(tokens, expert_ids, combine_weights, w_gate, w_up, w_down):
    tok_rows, width_part = tokens.shape
    top_count = expert_ids.shape[1]
    local_experts = w_gate.shape[0]
    owners = lax.axis_size("expert")
    experts = local_experts * owners
    expert_iota = lax.broadcasted_iota(jnp.int32, (1, 1, experts), 2)
    matches = (expert_ids[:, :, None] == expert_iota).astype(jnp.int32)
    per_token = jnp.sum(matches, axis=1)
    before = jnp.cumsum(per_token, axis=0) - per_token
    position = jnp.sum(matches * before[:, None, :], axis=2)
    slot_index = expert_ids * CAP + position
    slot_iota = lax.broadcasted_iota(jnp.int32, (experts * CAP, 1, 1), 0)
    placed = jnp.any(slot_index[None, :, :] == slot_iota, axis=2).astype(jnp.bfloat16)
    outgoing = jnp.dot(placed, tokens, preferred_element_type=jnp.float32).astype(jnp.bfloat16)
    incoming = lax.all_to_all(outgoing, "expert", split_axis=0, concat_axis=0, tiled=True)
    arrived = incoming.reshape(owners, local_experts, CAP, width_part)
    gate_part = jnp.einsum("hecd,edf->hecf", arrived, w_gate, preferred_element_type=jnp.float32)
    up_part = jnp.einsum("hecd,edf->hecf", arrived, w_up, preferred_element_type=jnp.float32)
    gate_sum, up_sum = (
        lax.psum_scatter(gate_part, "dp", scatter_dimension=0, tiled=True),
        lax.psum_scatter(up_part, "dp", scatter_dimension=0, tiled=True),
    )
    shares = (jax.nn.silu(gate_sum) * up_sum).astype(jnp.bfloat16)
    hidden = lax.all_gather(shares, "dp", axis=0, tiled=True)
    outputs = jnp.einsum(
        "hecf,efd->hecd", hidden, w_down, preferred_element_type=jnp.float32
    ).astype(jnp.bfloat16)
    returned = lax.all_to_all(
        outputs.reshape(owners * local_experts * CAP, width_part),
        "expert",
        split_axis=0,
        concat_axis=0,
        tiled=True,
    )
    picked = jnp.take(returned, slot_index.reshape(-1), axis=0).reshape(
        tok_rows, top_count, width_part
    )
    combined = jnp.sum(combine_weights[:, :, None] * picked.astype(jnp.float32), axis=1)
    return combined.astype(jnp.bfloat16)


def swap(value, axis, distance):
    size = lax.axis_size(axis)
    return lax.ppermute(value, axis, [(i, i ^ distance) for i in range(size)])


def project_kernel(top, group, rows, place, *refs):
    blocks = refs[: -7 - group // 2]
    w_gate, w_up, send = refs[-7 - group // 2 : -4 - group // 2]
    keeps = refs[-4 - group // 2 : -4]
    scale, slots, held, picked = refs[-4:]
    step = pl.program_id(0)
    member, first = place[0], place[1]
    depth = w_gate.shape[1]
    ff = w_gate.shape[2]
    tok_rows = blocks[0].shape[0]
    total = held.shape[0]

    @pl.when(step == 0)
    def _():
        for k, block in enumerate(blocks):
            held[k * tok_rows : (k + 1) * tok_rows, :] = block[...]
        meta = held[:, depth:].astype(jnp.float32)
        lane = lax.broadcasted_iota(jnp.int32, (1, LANES), 1)
        named = jnp.where(lane < group, first + (lane ^ member), -1).astype(jnp.float32)
        match = jnp.zeros((total, LANES), jnp.float32)
        for k in range(top):
            match = match + jnp.where(meta[:, k : k + 1] == named, 1.0, 0.0)
        row = lax.broadcasted_iota(jnp.int32, (total, total), 0)
        col = lax.broadcasted_iota(jnp.int32, (total, total), 1)
        earlier = jnp.where(row > col, 1.0, 0.0).astype(jnp.bfloat16)
        position = jnp.dot(
            earlier, match.astype(jnp.bfloat16), preferred_element_type=jnp.float32
        )
        position = jnp.where(match > 0.0, position, -1.0).astype(jnp.bfloat16)
        width = group * rows
        wide_row = lax.broadcasted_iota(jnp.int32, (LANES, width), 0)
        wide_col = lax.broadcasted_iota(jnp.int32, (LANES, width), 1)
        inside = (wide_col >= wide_row * rows) & (wide_col < (wide_row + 1) * rows)
        spread = jnp.where(inside, 1.0, 0.0).astype(jnp.bfloat16)
        wide = jnp.dot(position, spread, preferred_element_type=jnp.float32)
        slot = lax.broadcasted_iota(jnp.int32, (1, width), 1)
        for j in range(1, group):
            slot = slot - jnp.where(
                lax.broadcasted_iota(jnp.int32, (1, width), 1) >= j * rows, rows, 0
            )
        one_hot = jnp.where(wide == slot.astype(jnp.float32), 1.0, 0.0).astype(jnp.bfloat16)
        slots[...] = one_hot
        picked[...] = lax.dot_general(
            one_hot,
            held[...],
            (((0,), (0,)), ((), ())),
            preferred_element_type=jnp.float32,
        ).astype(jnp.bfloat16)
        own = picked[:rows, depth:].astype(jnp.float32)
        weight = (
            own[:, top : 2 * top] + own[:, 2 * top : 3 * top]
        ) + own[:, 3 * top : 4 * top]
        mine = (first + member).astype(jnp.float32)
        weight = jnp.sum(
            jnp.where(own[:, :top] == mine, weight, 0.0), axis=1, keepdims=True
        )
        scale[...] = jnp.broadcast_to(weight, scale.shape)

    half = group // 2
    relative = jnp.where(step < half, 2 * step + 1, 2 * (group - 1 - step))
    start = pl.multiple_of(relative * rows, 16)
    x = picked[pl.ds(start, rows), :depth]
    gate = jnp.dot(x, w_gate[0], preferred_element_type=jnp.float32)
    up = jnp.dot(x, w_up[0], preferred_element_type=jnp.float32)

    @pl.when(step < half)
    def _():
        send[pl.ds(step, 1), :, :ff] = gate.astype(send.dtype)[None]
        send[pl.ds(step, 1), :, ff:] = up.astype(send.dtype)[None]

    for j in range(half):

        @pl.when(step == group - 1 - j)
        def _(j=j):
            keeps[j][:, :ff] = gate
            keeps[j][:, ff:] = up


def project(blocks, place, w_gate, w_up, top, group, rows):
    depth, ff = w_gate.shape[1:]
    tok_rows, wide = blocks[0].shape
    total = tok_rows * len(blocks)
    half = group // 2

    def weight_index(step, place):
        relative = jnp.where(step < half, 2 * step + 1, 2 * (group - 1 - step))
        return place[2] + (relative ^ place[0]), 0, 0

    def whole(step, place):
        return 0, 0

    out_shape = (
        [jax.ShapeDtypeStruct((half, rows, 2 * ff), jnp.bfloat16)]
        + [jax.ShapeDtypeStruct((rows, 2 * ff), jnp.float32)] * half
        + [
            jax.ShapeDtypeStruct((rows, LANES), jnp.float32),
            jax.ShapeDtypeStruct((total, group * rows), jnp.bfloat16),
        ]
    )
    outs = pl.pallas_call(
        functools.partial(project_kernel, top, group, rows),
        out_shape=out_shape,
        grid_spec=pltpu.PrefetchScalarGridSpec(
            num_scalar_prefetch=1,
            grid=(group,),
            in_specs=[pl.BlockSpec((tok_rows, wide), whole)] * len(blocks)
            + [pl.BlockSpec((1, depth, ff), weight_index)] * 2,
            out_specs=[pl.BlockSpec((half, rows, 2 * ff), lambda step, place: (0, 0, 0))]
            + [pl.BlockSpec(s.shape, whole) for s in out_shape[1:]],
            scratch_shapes=[
                pltpu.VMEM((total, wide), jnp.bfloat16),
                pltpu.VMEM((group * rows, wide), jnp.bfloat16),
            ],
        ),
        compiler_params=pltpu.CompilerParams(vmem_limit_bytes=48 * 2**20),
        cost_estimate=pl.CostEstimate(
            flops=4 * group * rows * depth * ff,
            bytes_accessed=4 * group * depth * ff,
            transcendentals=0,
        ),
        name="project",
    )(place, *blocks, w_gate, w_up)
    return outs[0], outs[1 : 1 + half], outs[-2], outs[-1]


def down_kernel(count, chunks, rows, place, *refs):
    hidden = refs[:count]
    slots = refs[count : count + chunks]
    w_down = refs[count + chunks]
    outs = refs[count + chunks + 1 : -2]
    held, result = refs[-2:]
    step = pl.program_id(0)

    @pl.when(step == 0)
    def _():
        for k, part in enumerate(hidden):
            held[k * rows : (k + 1) * rows, :] = part[...]

    start = pl.multiple_of(step * rows, 16)
    result[pl.ds(start, rows), :] = jnp.dot(
        held[pl.ds(start, rows), :], w_down[0], preferred_element_type=jnp.float32
    ).astype(jnp.bfloat16)

    @pl.when(step == count - 1)
    def _():
        span = count * rows // chunks
        total = jnp.dot(slots[0][...], result[:span, :], preferred_element_type=jnp.float32)
        for c in range(1, chunks):
            total = total + jnp.dot(
                slots[c][...],
                result[c * span : (c + 1) * span, :],
                preferred_element_type=jnp.float32,
            )
        tok_rows = outs[0].shape[0]
        for k, out in enumerate(outs):
            out[...] = total[k * tok_rows : (k + 1) * tok_rows, :].astype(out.dtype)


def down(hidden, slots, place, w_down, part, columns, owners, group):
    rows, ff = hidden[0].shape
    count = len(hidden)
    total = slots[0].shape[0]
    tok_rows = total // owners

    def weight_index(step, place):
        return (step // group) * group + ((step % group) ^ place[0]), 0, part

    def whole(step, place):
        return 0, 0

    out_shape = [
        jax.ShapeDtypeStruct(
            (tok_rows, columns), jnp.float32 if k % NEAR == 0 else jnp.bfloat16
        )
        for k in range(owners)
    ]
    return pl.pallas_call(
        functools.partial(down_kernel, count, len(slots), rows),
        out_shape=out_shape,
        grid_spec=pltpu.PrefetchScalarGridSpec(
            num_scalar_prefetch=1,
            grid=(count,),
            in_specs=[pl.BlockSpec((rows, ff), whole)] * count
            + [pl.BlockSpec(s.shape, whole) for s in slots]
            + [pl.BlockSpec((1, ff, columns), weight_index)],
            out_specs=[pl.BlockSpec((tok_rows, columns), whole)] * owners,
            scratch_shapes=[
                pltpu.VMEM((count * rows, ff), jnp.bfloat16),
                pltpu.VMEM((count * rows, columns), jnp.bfloat16),
            ],
        ),
        compiler_params=pltpu.CompilerParams(vmem_limit_bytes=48 * 2**20),
        cost_estimate=pl.CostEstimate(
            flops=2 * count * rows * columns * (ff + total),
            bytes_accessed=2 * count * ff * columns,
            transcendentals=0,
        ),
        name="down",
    )(place, *hidden, *slots, w_down)


def split_three(value):
    high = value.astype(jnp.bfloat16)
    rest = value - high.astype(jnp.float32)
    middle = rest.astype(jnp.bfloat16)
    low = (rest - middle.astype(jnp.float32)).astype(jnp.bfloat16)
    return high, middle, low


def shards(tokens, expert_ids, combine_weights, w_gate, w_up, w_down):
    tok_rows, depth = tokens.shape
    top = expert_ids.shape[1]
    local_experts = w_gate.shape[0]
    ff = w_gate.shape[2]
    owners = lax.axis_size("expert")
    group = lax.axis_size("dp")
    rows = owners * CAP
    chunks = local_experts // group
    member = lax.axis_index("dp")
    first = lax.axis_index("expert") * local_experts
    places = [
        jnp.stack([member, first + c * group, jnp.int32(c * group)]) for c in range(chunks)
    ]

    meta = jnp.concatenate(
        (expert_ids.astype(jnp.bfloat16),) + split_three(combine_weights), axis=1
    )
    meta = jnp.pad(meta, ((0, 0), (0, LANES - meta.shape[1])))
    own = jnp.concatenate((tokens, meta), axis=1)
    blocks = {0: own}
    for far in range(NEAR, owners, NEAR):
        blocks[far] = swap(own, "expert", far)
    for far in range(0, owners, NEAR):
        for near in range(1, NEAR):
            blocks[far + near] = swap(blocks[far], "expert", near)
    ordered = [blocks[k] for k in range(owners)]

    hidden, slots = [], []
    for c in range(chunks):
        send, keeps, scale, one_hot = project(
            ordered, places[c], w_gate, w_up, top, group, rows
        )
        slots.append(one_hot)
        received = swap(send, "dp", 1).astype(jnp.float32)
        both = keeps[0] + received[0]
        for j in range(1, group // 2):
            part = (keeps[j] + received[j]).astype(jnp.bfloat16)
            both = both + swap(part, "dp", 2 * j).astype(jnp.float32)
        shares = jax.nn.silu(both[:, :ff]) * both[:, ff:] * scale[:, :1]
        gathered = {0: shares.astype(jnp.bfloat16)}
        for j in range(1, group // 2):
            gathered[2 * j] = swap(gathered[0], "dp", 2 * j)
        for j in range(group // 2):
            gathered[2 * j + 1] = swap(gathered[2 * j], "dp", 1)
        hidden += [gathered[k] for k in range(group)]

    columns = depth // COLUMN_PARTS
    done = []
    for part in range(COLUMN_PARTS):
        partial = down(hidden, slots, places[0], w_down, part, columns, owners, group)
        total = partial[0]
        sums = {}
        for far in range(NEAR, owners, NEAR):
            sums[far] = partial[far]
            for near in range(1, NEAR):
                sums[far] = sums[far] + swap(partial[far + near], "expert", near).astype(
                    jnp.float32
                )
        for near in range(1, NEAR):
            total = total + swap(partial[near], "expert", near).astype(jnp.float32)
        for far in range(NEAR, owners, NEAR):
            total = total + swap(sums[far].astype(jnp.bfloat16), "expert", far).astype(
                jnp.float32
            )
        done.append(total.astype(jnp.bfloat16))
    return jnp.concatenate(done, axis=1)


def fits(owners, group, tokens, expert_ids, w_gate):
    powers = all(k & (k - 1) == 0 for k in (owners, group))
    return (
        powers
        and owners >= NEAR
        and group >= 2
        and w_gate.shape[0] % group == 0
        and tokens.shape[0] % 16 == 0
        and (owners * CAP) % 16 == 0
        and owners * CAP < 256
        and owners * w_gate.shape[0] <= 256
        and 4 * expert_ids.shape[1] <= LANES
        and tokens.shape[1] % (COLUMN_PARTS * LANES) == 0
    )


def layer(tokens, expert_ids, combine_weights, w_gate, w_up, w_down):
    owners, group = lax.axis_size("expert"), lax.axis_size("dp")
    chosen = shards if fits(owners, group, tokens, expert_ids, w_gate) else plain_shards
    return chosen(tokens, expert_ids, combine_weights, w_gate, w_up, w_down)


def solution(mesh):
    placed = (
        P("expert", "dp"),
        P("expert", None),
        P("expert", None),
        P("expert", "dp", None),
        P("expert", "dp", None),
        P("expert", None, "dp"),
    )
    return jax.shard_map(
        layer, mesh=mesh, in_specs=placed, out_specs=P("expert", "dp"), check_vma=False
    )
```

```python
import functools
import math

import jax
import jax.numpy as jnp
from jax import lax
from jax.experimental import pallas as pl
from jax.experimental.pallas import tpu as pltpu
from jax.sharding import PartitionSpec as P

CAP = 10
NEAR = 4
LANES = 128
COLUMN_PARTS = 2


def plain_shards(tokens, expert_ids, combine_weights, w_gate, w_up, w_down):
    tok_rows, width_part = tokens.shape
    top_count = expert_ids.shape[1]
    local_experts = w_gate.shape[0]
    owners = lax.axis_size("expert")
    experts = local_experts * owners
    expert_iota = lax.broadcasted_iota(jnp.int32, (1, 1, experts), 2)
    matches = (expert_ids[:, :, None] == expert_iota).astype(jnp.int32)
    per_token = jnp.sum(matches, axis=1)
    before = jnp.cumsum(per_token, axis=0) - per_token
    position = jnp.sum(matches * before[:, None, :], axis=2)
    slot_index = expert_ids * CAP + position
    slot_iota = lax.broadcasted_iota(jnp.int32, (experts * CAP, 1, 1), 0)
    placed = jnp.any(slot_index[None, :, :] == slot_iota, axis=2).astype(jnp.bfloat16)
    outgoing = jnp.dot(placed, tokens, preferred_element_type=jnp.float32).astype(jnp.bfloat16)
    incoming = lax.all_to_all(outgoing, "expert", split_axis=0, concat_axis=0, tiled=True)
    arrived = incoming.reshape(owners, local_experts, CAP, width_part)
    gate_part = jnp.einsum("hecd,edf->hecf", arrived, w_gate, preferred_element_type=jnp.float32)
    up_part = jnp.einsum("hecd,edf->hecf", arrived, w_up, preferred_element_type=jnp.float32)
    gate_sum, up_sum = (
        lax.psum_scatter(gate_part, "dp", scatter_dimension=0, tiled=True),
        lax.psum_scatter(up_part, "dp", scatter_dimension=0, tiled=True),
    )
    shares = (jax.nn.silu(gate_sum) * up_sum).astype(jnp.bfloat16)
    hidden = lax.all_gather(shares, "dp", axis=0, tiled=True)
    outputs = jnp.einsum(
        "hecf,efd->hecd", hidden, w_down, preferred_element_type=jnp.float32
    ).astype(jnp.bfloat16)
    returned = lax.all_to_all(
        outputs.reshape(owners * local_experts * CAP, width_part),
        "expert",
        split_axis=0,
        concat_axis=0,
        tiled=True,
    )
    picked = jnp.take(returned, slot_index.reshape(-1), axis=0).reshape(
        tok_rows, top_count, width_part
    )
    combined = jnp.sum(combine_weights[:, :, None] * picked.astype(jnp.float32), axis=1)
    return combined.astype(jnp.bfloat16)


def swap(value, axis, distance):
    size = lax.axis_size(axis)
    return lax.ppermute(value, axis, [(i, i ^ distance) for i in range(size)])


def resident(value):
    return pltpu.with_memory_space_constraint(value, pltpu.VMEM)


def distant(value):
    return pltpu.with_memory_space_constraint(value, pltpu.HBM)


def in_vmem(count):
    return [pl.BlockSpec(memory_space=pltpu.VMEM)] * count


def anywhere(count):
    return [pl.BlockSpec(memory_space=pl.ANY)] * count


def in_hbm(count):
    return [pl.BlockSpec(memory_space=pltpu.HBM)] * count


def pack_kernel(tokens, ids, weights, packed):
    depth = tokens.shape[1]
    weight = weights[...]
    high = weight.astype(jnp.bfloat16).astype(jnp.float32)
    middle = (weight - high).astype(jnp.bfloat16).astype(jnp.float32)
    low = weight - high - middle
    rows = jnp.concatenate((ids[...].astype(jnp.float32), high, middle, low), axis=0)
    count = rows.shape[0]
    row = lax.broadcasted_iota(jnp.int32, (count, LANES), 0)
    col = lax.broadcasted_iota(jnp.int32, (count, LANES), 1)
    eye = jnp.where(row == col, 1.0, 0.0).astype(jnp.bfloat16)
    packed[:, :depth] = tokens[...]
    packed[:, depth:] = lax.dot_general(
        rows.astype(jnp.bfloat16),
        eye,
        (((0,), (0,)), ((), ())),
        preferred_element_type=jnp.float32,
    ).astype(jnp.bfloat16)


def pack(tokens, expert_ids, combine_weights):
    rows, depth = tokens.shape
    return pl.pallas_call(
        pack_kernel,
        out_shape=jax.ShapeDtypeStruct((rows, depth + LANES), jnp.bfloat16),
        in_specs=in_vmem(3),
        out_specs=pl.BlockSpec(memory_space=pltpu.VMEM),
        name="pack",
    )(tokens, expert_ids.T, combine_weights.T)


def visiting(group):
    return list(range(1, group, 2)) + list(range(0, group, 2))[::-1]


def load_kernel(starts, orders, place, *refs):
    count = len(starts)
    sources, targets = refs[:count], refs[count + 1 : 2 * count + 1]
    token, done = refs[-2:]
    copies = []
    for k in range(max(map(len, orders))):
        for i in range(count):
            if k < len(orders[i]):
                copies.append(
                    pltpu.make_async_copy(
                        sources[i].at[starts[i] + (orders[i][k] ^ place[0])],
                        targets[i].at[k],
                        done.at[i, k],
                    )
                )
                copies[-1].start()
    token[...] = jnp.zeros_like(token)
    for copy in copies:
        copy.wait()


def load(weights, starts, orders, place, after):
    count = len(weights)
    shapes = [
        pltpu.VMEM((len(order),) + w.shape[1:], w.dtype) for w, order in zip(weights, orders)
    ]
    size = sum(2 * math.prod(shape.shape) for shape in shapes)
    *loaded, token = pl.pallas_call(
        functools.partial(load_kernel, starts, orders),
        out_shape=shapes + [jax.ShapeDtypeStruct((8, LANES), jnp.float32)],
        in_specs=[pl.BlockSpec(memory_space=pltpu.SMEM)] + in_hbm(count) + anywhere(1),
        out_specs=in_vmem(count + 1),
        scratch_shapes=[pltpu.SemaphoreType.DMA((count, max(map(len, orders))))],
        compiler_params=pltpu.CompilerParams(vmem_limit_bytes=2 * 2**20),
        cost_estimate=pl.CostEstimate(flops=0, bytes_accessed=size, transcendentals=0),
        name="load",
    )(place, *map(distant, weights), after)
    return loaded, token


def merge_kernel(half, *refs):
    received, keeps, parts, base = refs[0], refs[1 : 1 + half], refs[1 + half : -1], refs[-1]
    base[...] = keeps[0][...] + received[0].astype(jnp.float32)
    for j, part in enumerate(parts):
        part[...] = (keeps[j + 1][...] + received[j + 1].astype(jnp.float32)).astype(part.dtype)


def merge(received, keeps):
    half = len(keeps)
    shape = keeps[0].shape
    *parts, base = pl.pallas_call(
        functools.partial(merge_kernel, half),
        out_shape=[jax.ShapeDtypeStruct(shape, jnp.bfloat16)] * (half - 1)
        + [jax.ShapeDtypeStruct(shape, jnp.float32)],
        in_specs=in_vmem(1 + half),
        out_specs=in_vmem(half),
        compiler_params=pltpu.CompilerParams(vmem_limit_bytes=4 * 2**20),
        name="merge",
    )(received, *keeps)
    return parts, base


def route(blocks, held, picked, scale, slots, place, top, group, rows):
    depth = held.shape[1] - LANES
    tok_rows = blocks[0].shape[0]
    total = held.shape[0]
    member, first = place[0], place[1]
    for k, block in enumerate(blocks):
        held[k * tok_rows : (k + 1) * tok_rows, :] = block[...]
    meta = held[:, depth:].astype(jnp.float32)
    lane = lax.broadcasted_iota(jnp.int32, (1, LANES), 1)
    named = jnp.where(lane < group, first + (lane ^ member), -1).astype(jnp.float32)
    match = jnp.zeros((total, LANES), jnp.float32)
    for k in range(top):
        match = match + jnp.where(meta[:, k : k + 1] == named, 1.0, 0.0)
    row = lax.broadcasted_iota(jnp.int32, (total, total), 0)
    col = lax.broadcasted_iota(jnp.int32, (total, total), 1)
    earlier = jnp.where(row > col, 1.0, 0.0).astype(jnp.bfloat16)
    position = jnp.dot(earlier, match.astype(jnp.bfloat16), preferred_element_type=jnp.float32)
    position = jnp.where(match > 0.0, position, -1.0).astype(jnp.bfloat16)
    width = group * rows
    wide_row = lax.broadcasted_iota(jnp.int32, (LANES, width), 0)
    wide_col = lax.broadcasted_iota(jnp.int32, (LANES, width), 1)
    inside = (wide_col >= wide_row * rows) & (wide_col < (wide_row + 1) * rows)
    spread = jnp.where(inside, 1.0, 0.0).astype(jnp.bfloat16)
    wide = jnp.dot(position, spread, preferred_element_type=jnp.float32)
    number = lax.broadcasted_iota(jnp.int32, (1, width), 1)
    slot = number
    for j in range(1, group):
        slot = slot - jnp.where(number >= j * rows, rows, 0)
    one_hot = jnp.where(wide == slot.astype(jnp.float32), 1.0, 0.0).astype(jnp.bfloat16)
    slots[...] = one_hot
    picked[...] = lax.dot_general(
        one_hot, held[...], (((0,), (0,)), ((), ())), preferred_element_type=jnp.float32
    ).astype(jnp.bfloat16)
    own = picked[:rows, depth:].astype(jnp.float32)
    weight = (own[:, top : 2 * top] + own[:, 2 * top : 3 * top]) + own[:, 3 * top : 4 * top]
    mine = (first + member).astype(jnp.float32)
    weight = jnp.sum(jnp.where(own[:, :top] == mine, weight, 0.0), axis=1, keepdims=True)
    scale[...] = jnp.broadcast_to(weight, scale.shape)


def project_kernel(top, group, rows, owners, ready, place, *refs):
    half = group // 2
    blocks = refs[:owners]
    near = refs[owners : owners + 2] if ready else ()
    refs = refs[owners + len(near) :]
    far, send, keeps = refs[:2], refs[3], refs[4 : 4 + half]
    scale, slots, held, picked = refs[4 + half : 8 + half]
    order = visiting(group)
    copies = {}
    if ready < group:
        *buffers, done = refs[8 + half :]
        for k in range(ready, group):
            for i in range(2):
                copies[i, k] = pltpu.make_async_copy(
                    far[i].at[place[2] + (order[k] ^ place[0])],
                    buffers[i].at[k - ready],
                    done.at[i, k - ready],
                )
                copies[i, k].start()
    route(blocks, held, picked, scale, slots, place, top, group, rows)
    depth, ff = far[0].shape[1:]
    for k, number in enumerate(order):
        for i in range(2):
            if k >= ready:
                copies[i, k].wait()
            part = jnp.dot(
                picked[number * rows : (number + 1) * rows, :depth],
                near[i][k] if k < ready else buffers[i][k - ready],
                preferred_element_type=jnp.float32,
            )
            if number % 2:
                send[number // 2, :, i * ff : (i + 1) * ff] = part.astype(send.dtype)
            else:
                keeps[number // 2][:, i * ff : (i + 1) * ff] = part


def project(blocks, place, near, weights, after, top, group, rows):
    ready = near[0].shape[0] if near else 0
    depth, ff = weights[0].shape[1:]
    tok_rows, wide = blocks[0].shape
    owners = len(blocks)
    total = tok_rows * owners
    half = group // 2
    out_shape = (
        [jax.ShapeDtypeStruct((half, rows, 2 * ff), jnp.bfloat16)]
        + [jax.ShapeDtypeStruct((rows, 2 * ff), jnp.float32)] * half
        + [
            jax.ShapeDtypeStruct((rows, LANES), jnp.float32),
            jax.ShapeDtypeStruct((total, group * rows), jnp.bfloat16),
        ]
    )
    scratch = [
        pltpu.VMEM((total, wide), jnp.bfloat16),
        pltpu.VMEM((group * rows, wide), jnp.bfloat16),
    ]
    streamed = group - ready
    if streamed:
        scratch += [pltpu.VMEM((streamed, depth, ff), jnp.bfloat16)] * 2
        scratch += [pltpu.SemaphoreType.DMA((2, streamed))]
    outs = pl.pallas_call(
        functools.partial(project_kernel, top, group, rows, owners, ready),
        out_shape=out_shape,
        in_specs=[pl.BlockSpec(memory_space=pltpu.SMEM)]
        + in_vmem(owners + len(near))
        + in_hbm(2)
        + anywhere(1),
        out_specs=in_vmem(len(out_shape)),
        scratch_shapes=scratch,
        compiler_params=pltpu.CompilerParams(
            vmem_limit_bytes=8 * 2**20 + streamed * depth * ff * 4
        ),
        cost_estimate=pl.CostEstimate(
            flops=4 * group * rows * depth * ff,
            bytes_accessed=4 * group * depth * ff,
            transcendentals=0,
        ),
        name="project",
    )(place, *blocks, *map(resident, near), *map(distant, weights), after)
    return outs[0], outs[1 : 1 + half], outs[-2], outs[-1]


def down_kernel(*refs):
    *hidden, weights, slots, _, total, result = refs
    rows = hidden[0].shape[0]
    for k, part in enumerate(hidden):
        result[k * rows : (k + 1) * rows, :] = jnp.dot(
            part[...], weights[k], preferred_element_type=jnp.float32
        ).astype(jnp.bfloat16)
    total[...] = jnp.dot(slots[...], result[...], preferred_element_type=jnp.float32)


def down(hidden, weights, slots, after):
    rows, ff = hidden[0].shape
    count, columns = len(hidden), weights.shape[2]
    total = slots.shape[0]
    return pl.pallas_call(
        down_kernel,
        out_shape=jax.ShapeDtypeStruct((total, columns), jnp.float32),
        in_specs=in_vmem(count + 2) + anywhere(1),
        out_specs=pl.BlockSpec(memory_space=pltpu.VMEM),
        scratch_shapes=[pltpu.VMEM((count * rows, columns), jnp.bfloat16)],
        compiler_params=pltpu.CompilerParams(vmem_limit_bytes=8 * 2**20),
        cost_estimate=pl.CostEstimate(
            flops=2 * count * rows * columns * (ff + total),
            bytes_accessed=2 * count * ff * columns,
            transcendentals=0,
        ),
        name="down",
    )(*hidden, resident(weights), slots, after)


def finish_kernel(count, chunks, start, columns, *refs):
    hidden, weights, slots = refs[:count], refs[count], refs[count + 1]
    others = refs[count + 2 : count + 1 + chunks]
    outs, result = refs[count + 1 + chunks : -1], refs[-1]
    rows = hidden[0].shape[0]
    for k, part in enumerate(hidden):
        result[k * rows : (k + 1) * rows, :] = jnp.dot(
            part[...],
            weights[k, :, start : start + columns],
            preferred_element_type=jnp.float32,
        ).astype(jnp.bfloat16)
    total = jnp.dot(slots[...], result[...], preferred_element_type=jnp.float32)
    for other in others:
        total = total + other[:, start : start + columns]
    tok_rows = outs[0].shape[0]
    for k, out in enumerate(outs):
        out[...] = total[k * tok_rows : (k + 1) * tok_rows, :].astype(out.dtype)


def finish(hidden, weights, slots, others, start, columns, owners):
    rows, ff = hidden[0].shape
    count = len(hidden)
    total = slots.shape[0]
    out_shape = [
        jax.ShapeDtypeStruct(
            (total // owners, columns), jnp.float32 if k % NEAR == 0 else jnp.bfloat16
        )
        for k in range(owners)
    ]
    return pl.pallas_call(
        functools.partial(finish_kernel, count, len(others) + 1, start, columns),
        out_shape=out_shape,
        in_specs=in_vmem(count + 2 + len(others)),
        out_specs=in_vmem(owners),
        scratch_shapes=[pltpu.VMEM((count * rows, columns), jnp.bfloat16)],
        compiler_params=pltpu.CompilerParams(vmem_limit_bytes=8 * 2**20),
        cost_estimate=pl.CostEstimate(
            flops=2 * count * rows * columns * (ff + total),
            bytes_accessed=2 * count * ff * columns,
            transcendentals=0,
        ),
        name="finish",
    )(*hidden, resident(weights), slots, *others)


def activate_kernel(*refs):
    *sums, scale, out = refs
    both = sums[0][...]
    for part in sums[1:]:
        both = both + part[...].astype(jnp.float32)
    ff = out.shape[1]
    out[...] = (jax.nn.silu(both[:, :ff]) * both[:, ff:] * scale[:, :1]).astype(out.dtype)


def activate(base, arrived, scale):
    rows, wide = base.shape
    return pl.pallas_call(
        activate_kernel,
        out_shape=jax.ShapeDtypeStruct((rows, wide // 2), jnp.bfloat16),
        in_specs=in_vmem(2 + len(arrived)),
        out_specs=pl.BlockSpec(memory_space=pltpu.VMEM),
        compiler_params=pltpu.CompilerParams(vmem_limit_bytes=4 * 2**20),
        name="activate",
    )(base, *arrived, scale)


def spread(own, group):
    gathered = {0: own, 1: swap(own, "dp", 1)}
    for j in range(2, group, 2):
        gathered[j] = swap(own, "dp", j)
    return gathered


def complete(gathered, group):
    for j in range(2, group, 2):
        gathered[j + 1] = swap(gathered[j], "dp", 1)
    return [gathered[k] for k in range(group)]


def shards(tokens, expert_ids, combine_weights, w_gate, w_up, w_down):
    tok_rows, depth = tokens.shape
    top = expert_ids.shape[1]
    local_experts = w_gate.shape[0]
    ff = w_gate.shape[2]
    owners = lax.axis_size("expert")
    group = lax.axis_size("dp")
    rows = owners * CAP
    chunks = local_experts // group
    member = lax.axis_index("dp")
    first = lax.axis_index("expert") * local_experts
    places = [
        jnp.stack([member, first + c * group, jnp.int32(c * group)]) for c in range(chunks)
    ]

    order = visiting(group)
    own = pack(tokens, expert_ids, combine_weights)
    far_blocks = {far: swap(own, "expert", far) for far in range(NEAR, owners, NEAR)}
    near_blocks = {near: swap(own, "expert", near) for near in range(1, NEAR)}
    (gate_ready,), token = load((w_gate,), (0,), (order,), places[0], own)
    far_blocks, token = lax.optimization_barrier((far_blocks, token))
    blocks = {0: own} | near_blocks | far_blocks
    for far in far_blocks:
        for near in range(1, NEAR):
            blocks[far + near] = swap(blocks[far], "expert", near)
    ordered = [blocks[k] for k in range(owners)]
    (up_ready,), _ = load((w_up,), (0,), (order,), places[0], token)

    hidden, slots = [], []
    after = token
    for c in range(chunks):
        near = (gate_ready, up_ready) if c == 0 else ()
        send, keeps, scale, one_hot = project(
            ordered, places[c], near, (w_gate, w_up), after, top, group, rows
        )
        slots.append(one_hot)
        if c > 0:
            send, arrived = lax.optimization_barrier((send, arrived))
            hidden.append(spread(activate(base, arrived, old_scale), group))
        parts, base = merge(swap(send, "dp", 1), keeps)
        old_scale = scale
        arrived = [swap(part, "dp", 2 * j) for j, part in enumerate(parts, 1)]
        after = parts[0] if parts else base
    starts = tuple(range(0, local_experts, group))
    members = (list(range(group)),) * chunks
    down_weights, token = load((w_down,) * chunks, starts, members, places[0], after)
    arrived, hidden, token = lax.optimization_barrier((arrived, hidden, token))
    last = spread(activate(base, arrived, old_scale), group)
    hidden = [complete(gathered, group) for gathered in hidden]
    others = [down(hidden[c], down_weights[c], slots[c], token) for c in range(chunks - 1)]
    if others:
        last, others = lax.optimization_barrier((last, others))
    hidden.append(complete(last, group))
    columns = depth // COLUMN_PARTS
    done = []
    for start in range(0, depth, columns):
        partial = finish(
            hidden[-1], down_weights[-1], slots[-1], others, start, columns, owners
        )
        total = partial[0]
        sums = {}
        for far in range(NEAR, owners, NEAR):
            sums[far] = partial[far]
            for near in range(1, NEAR):
                sums[far] = sums[far] + swap(partial[far + near], "expert", near).astype(
                    jnp.float32
                )
        for near in range(1, NEAR):
            total = total + swap(partial[near], "expert", near).astype(jnp.float32)
        for far in range(NEAR, owners, NEAR):
            total = total + swap(sums[far].astype(jnp.bfloat16), "expert", far).astype(
                jnp.float32
            )
        done.append(total.astype(jnp.bfloat16))
    return jnp.concatenate(done, axis=1)


def fits(owners, group, tokens, expert_ids, w_gate):
    powers = all(k & (k - 1) == 0 for k in (owners, group))
    return (
        powers
        and owners >= NEAR
        and group >= 2
        and w_gate.shape[0] % group == 0
        and tokens.shape[0] % 16 == 0
        and (owners * CAP) % 16 == 0
        and owners * CAP < 256
        and owners * w_gate.shape[0] <= 256
        and 4 * expert_ids.shape[1] <= LANES
        and tokens.shape[1] % (COLUMN_PARTS * LANES) == 0
    )


def layer(tokens, expert_ids, combine_weights, w_gate, w_up, w_down):
    owners, group = lax.axis_size("expert"), lax.axis_size("dp")
    chosen = shards if fits(owners, group, tokens, expert_ids, w_gate) else plain_shards
    return chosen(tokens, expert_ids, combine_weights, w_gate, w_up, w_down)


def solution(mesh):
    placed = (
        P("expert", "dp"),
        P("expert", None),
        P("expert", None),
        P("expert", "dp", None),
        P("expert", "dp", None),
        P("expert", None, "dp"),
    )
    return jax.shard_map(
        layer, mesh=mesh, in_specs=placed, out_specs=P("expert", "dp"), check_vma=False
    )
```

```python
import functools
import math

import jax
import jax.numpy as jnp
from jax import lax
from jax.experimental import pallas as pl
from jax.experimental.pallas import tpu as pltpu
from jax.sharding import PartitionSpec as P

CAP = 10
NEAR = 4
LANES = 128
PIECES = 4
BASE_VMEM = 5 * 2**20
COLUMN_PARTS = 2


def plain_shards(tokens, expert_ids, combine_weights, w_gate, w_up, w_down):
    tok_rows, width_part = tokens.shape
    top_count = expert_ids.shape[1]
    local_experts = w_gate.shape[0]
    owners = lax.axis_size("expert")
    experts = local_experts * owners
    expert_iota = lax.broadcasted_iota(jnp.int32, (1, 1, experts), 2)
    matches = (expert_ids[:, :, None] == expert_iota).astype(jnp.int32)
    per_token = jnp.sum(matches, axis=1)
    before = jnp.cumsum(per_token, axis=0) - per_token
    position = jnp.sum(matches * before[:, None, :], axis=2)
    slot_index = expert_ids * CAP + position
    slot_iota = lax.broadcasted_iota(jnp.int32, (experts * CAP, 1, 1), 0)
    placed = jnp.any(slot_index[None, :, :] == slot_iota, axis=2).astype(jnp.bfloat16)
    outgoing = jnp.dot(placed, tokens, preferred_element_type=jnp.float32).astype(jnp.bfloat16)
    incoming = lax.all_to_all(outgoing, "expert", split_axis=0, concat_axis=0, tiled=True)
    arrived = incoming.reshape(owners, local_experts, CAP, width_part)
    gate_part = jnp.einsum("hecd,edf->hecf", arrived, w_gate, preferred_element_type=jnp.float32)
    up_part = jnp.einsum("hecd,edf->hecf", arrived, w_up, preferred_element_type=jnp.float32)
    gate_sum, up_sum = (
        lax.psum_scatter(gate_part, "dp", scatter_dimension=0, tiled=True),
        lax.psum_scatter(up_part, "dp", scatter_dimension=0, tiled=True),
    )
    shares = (jax.nn.silu(gate_sum) * up_sum).astype(jnp.bfloat16)
    hidden = lax.all_gather(shares, "dp", axis=0, tiled=True)
    outputs = jnp.einsum(
        "hecf,efd->hecd", hidden, w_down, preferred_element_type=jnp.float32
    ).astype(jnp.bfloat16)
    returned = lax.all_to_all(
        outputs.reshape(owners * local_experts * CAP, width_part),
        "expert",
        split_axis=0,
        concat_axis=0,
        tiled=True,
    )
    picked = jnp.take(returned, slot_index.reshape(-1), axis=0).reshape(
        tok_rows, top_count, width_part
    )
    combined = jnp.sum(combine_weights[:, :, None] * picked.astype(jnp.float32), axis=1)
    return combined.astype(jnp.bfloat16)


def swap(value, axis, distance):
    size = lax.axis_size(axis)
    return lax.ppermute(value, axis, [(i, i ^ distance) for i in range(size)])


def resident(value):
    return pltpu.with_memory_space_constraint(value, pltpu.VMEM)


def distant(value):
    return pltpu.with_memory_space_constraint(value, pltpu.HBM)


def in_vmem(count):
    return [pl.BlockSpec(memory_space=pltpu.VMEM)] * count


def anywhere(count):
    return [pl.BlockSpec(memory_space=pl.ANY)] * count


def in_hbm(count):
    return [pl.BlockSpec(memory_space=pltpu.HBM)] * count


def pack_kernel(tokens, ids, weights, packed):
    depth = tokens.shape[1]
    weight = weights[...]
    high = weight.astype(jnp.bfloat16).astype(jnp.float32)
    middle = (weight - high).astype(jnp.bfloat16).astype(jnp.float32)
    low = weight - high - middle
    rows = jnp.concatenate((ids[...].astype(jnp.float32), high, middle, low), axis=0)
    count = rows.shape[0]
    row = lax.broadcasted_iota(jnp.int32, (count, LANES), 0)
    col = lax.broadcasted_iota(jnp.int32, (count, LANES), 1)
    eye = jnp.where(row == col, 1.0, 0.0).astype(jnp.bfloat16)
    packed[:, :depth] = tokens[...]
    packed[:, depth:] = lax.dot_general(
        rows.astype(jnp.bfloat16),
        eye,
        (((0,), (0,)), ((), ())),
        preferred_element_type=jnp.float32,
    ).astype(jnp.bfloat16)


def pack(tokens, expert_ids, combine_weights):
    rows, depth = tokens.shape
    return pl.pallas_call(
        pack_kernel,
        out_shape=jax.ShapeDtypeStruct((rows, depth + LANES), jnp.bfloat16),
        in_specs=in_vmem(3),
        out_specs=pl.BlockSpec(memory_space=pltpu.VMEM),
        name="pack",
    )(tokens, expert_ids.T, combine_weights.T)


def visiting(group):
    return list(range(1, group, 2)) + list(range(0, group, 2))[::-1]


def load_kernel(starts, orders, place, *refs):
    count = len(starts)
    sources, targets = refs[:count], refs[count + 1 : 2 * count + 1]
    token, done = refs[-2:]
    copies = []
    for k in range(max(map(len, orders))):
        for i in range(count):
            if k < len(orders[i]):
                expert = starts[i] + (orders[i][k] ^ place[0])
                rows = targets[i].shape[1] // PIECES
                for j in range(PIECES):
                    copies.append(
                        pltpu.make_async_copy(
                            sources[i].at[expert, pl.ds(j * rows, rows)],
                            targets[i].at[k, pl.ds(j * rows, rows)],
                            done.at[i, k, j],
                        )
                    )
                    copies[-1].start()
    token[...] = jnp.zeros_like(token)
    for copy in copies:
        copy.wait()


def load(weights, starts, orders, place, after):
    count = len(weights)
    shapes = [
        pltpu.VMEM((len(order),) + w.shape[1:], w.dtype) for w, order in zip(weights, orders)
    ]
    size = sum(2 * math.prod(shape.shape) for shape in shapes)
    *loaded, token = pl.pallas_call(
        functools.partial(load_kernel, starts, orders),
        out_shape=shapes + [jax.ShapeDtypeStruct((8, LANES), jnp.float32)],
        in_specs=[pl.BlockSpec(memory_space=pltpu.SMEM)] + in_hbm(count) + anywhere(1),
        out_specs=in_vmem(count + 1),
        scratch_shapes=[pltpu.SemaphoreType.DMA((count, max(map(len, orders)), PIECES))],
        compiler_params=pltpu.CompilerParams(vmem_limit_bytes=2 * 2**20),
        cost_estimate=pl.CostEstimate(flops=0, bytes_accessed=size, transcendentals=0),
        name="load",
    )(place, *map(distant, weights), after)
    return loaded, token


def merge_kernel(half, *refs):
    received, keeps, parts, base = refs[0], refs[1 : 1 + half], refs[1 + half : -1], refs[-1]
    base[...] = keeps[0][...] + received[0].astype(jnp.float32)
    for j, part in enumerate(parts):
        part[...] = (keeps[j + 1][...] + received[j + 1].astype(jnp.float32)).astype(part.dtype)


def merge(received, keeps):
    half = len(keeps)
    shape = keeps[0].shape
    *parts, base = pl.pallas_call(
        functools.partial(merge_kernel, half),
        out_shape=[jax.ShapeDtypeStruct(shape, jnp.bfloat16)] * (half - 1)
        + [jax.ShapeDtypeStruct(shape, jnp.float32)],
        in_specs=in_vmem(1 + half),
        out_specs=in_vmem(half),
        compiler_params=pltpu.CompilerParams(vmem_limit_bytes=4 * 2**20),
        name="merge",
    )(received, *keeps)
    return parts, base


def route(blocks, held, picked, scale, slots, place, top, group, rows):
    depth = held.shape[1] - LANES
    tok_rows = blocks[0].shape[0]
    total = held.shape[0]
    member, first = place[0], place[1]
    for k, block in enumerate(blocks):
        held[k * tok_rows : (k + 1) * tok_rows, :] = block[...]
    meta = held[:, depth:].astype(jnp.float32)
    lane = lax.broadcasted_iota(jnp.int32, (1, LANES), 1)
    named = jnp.where(lane < group, first + (lane ^ member), -1).astype(jnp.float32)
    match = jnp.zeros((total, LANES), jnp.float32)
    for k in range(top):
        match = match + jnp.where(meta[:, k : k + 1] == named, 1.0, 0.0)
    row = lax.broadcasted_iota(jnp.int32, (total, total), 0)
    col = lax.broadcasted_iota(jnp.int32, (total, total), 1)
    earlier = jnp.where(row > col, 1.0, 0.0).astype(jnp.bfloat16)
    position = jnp.dot(earlier, match.astype(jnp.bfloat16), preferred_element_type=jnp.float32)
    position = jnp.where(match > 0.0, position, -1.0).astype(jnp.bfloat16)
    width = group * rows
    wide_row = lax.broadcasted_iota(jnp.int32, (LANES, width), 0)
    wide_col = lax.broadcasted_iota(jnp.int32, (LANES, width), 1)
    inside = (wide_col >= wide_row * rows) & (wide_col < (wide_row + 1) * rows)
    spread = jnp.where(inside, 1.0, 0.0).astype(jnp.bfloat16)
    wide = jnp.dot(position, spread, preferred_element_type=jnp.float32)
    number = lax.broadcasted_iota(jnp.int32, (1, width), 1)
    slot = number
    for j in range(1, group):
        slot = slot - jnp.where(number >= j * rows, rows, 0)
    one_hot = jnp.where(wide == slot.astype(jnp.float32), 1.0, 0.0).astype(jnp.bfloat16)
    slots[...] = one_hot
    step = 3 * LANES
    for begin in range(0, held.shape[1], step):
        end = min(begin + step, held.shape[1])
        picked[:, begin:end] = lax.dot_general(
            one_hot,
            held[:, begin:end],
            (((0,), (0,)), ((), ())),
            preferred_element_type=jnp.float32,
        ).astype(jnp.bfloat16)
    own = picked[:rows, depth:].astype(jnp.float32)
    weight = (own[:, top : 2 * top] + own[:, 2 * top : 3 * top]) + own[:, 3 * top : 4 * top]
    mine = (first + member).astype(jnp.float32)
    weight = jnp.sum(jnp.where(own[:, :top] == mine, weight, 0.0), axis=1, keepdims=True)
    scale[...] = jnp.broadcast_to(weight, scale.shape)


def project_kernel(top, group, rows, numbers, owners, stream, ahead, place, *refs):
    refs = list(refs)

    def take(count):
        taken, refs[:count] = refs[:count], []
        return taken

    blocks, weights = take(owners), take(2)
    near = weights[0].shape[0]
    streamed = len(numbers) - near
    far = take(2) if streamed or ahead else []
    take(1)
    half = group // 2
    send, keeps = take(1)[0], take(half)
    scale, slots = take(2)
    targets = take(2) if ahead else []
    held, picked = take(2)
    copies = {}
    if streamed:
        buffers, arrivals = take(2), take(1)[0]
        for k in range(streamed):
            for i in range(2):
                copies[i, k] = pltpu.make_async_copy(
                    far[i].at[stream + (numbers[near + k] ^ place[0])],
                    buffers[i].at[k],
                    arrivals.at[i, k],
                )
                copies[i, k].start()
    waiting = []
    if ahead:
        fetched = take(1)[0]
        for i in range(2):
            for k in range(ahead):
                waiting.append(
                    pltpu.make_async_copy(
                        far[i].at[stream + group + (numbers[k] ^ place[0])],
                        targets[i].at[k],
                        fetched.at[i, k],
                    )
                )
                waiting[-1].start()
    depth, ff = weights[0].shape[1:]

    @pl.when(place[0] >= 0)
    def _():
        route(blocks, held, picked, scale, slots, place, top, group, rows)
        for k, number in enumerate(numbers):
            for i in range(2):
                if k >= near:
                    copies[i, k - near].wait()
                part = jnp.dot(
                    picked[number * rows : (number + 1) * rows, :depth],
                    weights[i][k] if k < near else buffers[i][k - near],
                    preferred_element_type=jnp.float32,
                )
                if number % 2:
                    send[number // 2, :, i * ff : (i + 1) * ff] = part.astype(send.dtype)
                else:
                    keeps[number // 2][:, i * ff : (i + 1) * ff] = part

    for copy in waiting:
        copy.wait()


def project(blocks, place, weights, pair, stream, numbers, ahead, after, top, group, rows):
    depth, ff = weights[0].shape[1:]
    owners = len(blocks)
    tok_rows, wide = blocks[0].shape
    total = tok_rows * owners
    half = group // 2
    streamed = len(numbers) - weights[0].shape[0]
    pair = list(pair) if streamed or ahead else []
    out_shape = [jax.ShapeDtypeStruct((half, rows, 2 * ff), jnp.bfloat16)]
    out_shape += [jax.ShapeDtypeStruct((rows, 2 * ff), jnp.float32)] * half
    out_shape += [
        jax.ShapeDtypeStruct((rows, LANES), jnp.float32),
        jax.ShapeDtypeStruct((total, group * rows), jnp.bfloat16),
    ]
    out_shape += [pltpu.VMEM((ahead, depth, ff), jnp.bfloat16)] * (2 * (ahead > 0))
    scratch = [
        pltpu.VMEM((total, wide), jnp.bfloat16),
        pltpu.VMEM((group * rows, wide), jnp.bfloat16),
    ]
    if streamed:
        scratch += [pltpu.VMEM((streamed, depth, ff), jnp.bfloat16)] * 2
        scratch += [pltpu.SemaphoreType.DMA((2, streamed))]
    if ahead:
        scratch += [pltpu.SemaphoreType.DMA((2, ahead))]
    return pl.pallas_call(
        functools.partial(project_kernel, top, group, rows, numbers, owners, stream, ahead),
        out_shape=out_shape,
        in_specs=[pl.BlockSpec(memory_space=pltpu.SMEM)]
        + in_vmem(owners + 2)
        + in_hbm(len(pair))
        + anywhere(1),
        out_specs=in_vmem(len(out_shape)),
        scratch_shapes=scratch,
        compiler_params=pltpu.CompilerParams(
            vmem_limit_bytes=BASE_VMEM + streamed * depth * ff * 4
        ),
        cost_estimate=pl.CostEstimate(
            flops=4 * len(numbers) * rows * depth * ff,
            bytes_accessed=4 * len(numbers) * depth * ff,
            transcendentals=0,
        ),
        name="project",
    )(place, *blocks, *map(resident, weights), *map(distant, pair), after)


def down_kernel(count, *refs):
    hidden, weights, slots = refs[:count], refs[count], refs[count + 1]
    total, result = refs[-2:]
    rows = hidden[0].shape[0]
    for k, part in enumerate(hidden):
        result[k * rows : (k + 1) * rows, :] = jnp.dot(
            part[...], weights[k], preferred_element_type=jnp.float32
        ).astype(jnp.bfloat16)
    total[...] = jnp.dot(slots[...], result[...], preferred_element_type=jnp.float32)


def down(hidden, weights, slots, after):
    rows, ff = hidden[0].shape
    count, columns = len(hidden), weights.shape[2]
    total = slots.shape[0]
    return pl.pallas_call(
        functools.partial(down_kernel, count),
        out_shape=jax.ShapeDtypeStruct((total, columns), jnp.float32),
        in_specs=in_vmem(count + 2) + anywhere(len(after)),
        out_specs=pl.BlockSpec(memory_space=pltpu.VMEM),
        scratch_shapes=[pltpu.VMEM((count * rows, columns), jnp.bfloat16)],
        compiler_params=pltpu.CompilerParams(vmem_limit_bytes=6 * 2**20),
        cost_estimate=pl.CostEstimate(
            flops=2 * count * rows * columns * (ff + total),
            bytes_accessed=2 * count * ff * columns,
            transcendentals=0,
        ),
        name="down",
    )(*hidden, resident(weights), slots, *after)


def finish_kernel(count, chunks, start, columns, *refs):
    hidden, weights, slots = refs[:count], refs[count], refs[count + 1]
    others = refs[count + 2 : count + 1 + chunks]
    outs, result = refs[count + 1 + chunks : -1], refs[-1]
    rows = hidden[0].shape[0]
    for k, part in enumerate(hidden):
        result[k * rows : (k + 1) * rows, :] = jnp.dot(
            part[...],
            weights[k, :, start : start + columns],
            preferred_element_type=jnp.float32,
        ).astype(jnp.bfloat16)
    total = jnp.dot(slots[...], result[...], preferred_element_type=jnp.float32)
    for other in others:
        total = total + other[:, start : start + columns]
    tok_rows = outs[0].shape[0]
    for k, out in enumerate(outs):
        out[...] = total[k * tok_rows : (k + 1) * tok_rows, :].astype(out.dtype)


def finish(hidden, weights, slots, others, start, columns, owners):
    rows, ff = hidden[0].shape
    count = len(hidden)
    total = slots.shape[0]
    out_shape = [
        jax.ShapeDtypeStruct(
            (total // owners, columns), jnp.float32 if k % NEAR == 0 else jnp.bfloat16
        )
        for k in range(owners)
    ]
    return pl.pallas_call(
        functools.partial(finish_kernel, count, len(others) + 1, start, columns),
        out_shape=out_shape,
        in_specs=in_vmem(count + 2 + len(others)),
        out_specs=in_vmem(owners),
        scratch_shapes=[pltpu.VMEM((count * rows, columns), jnp.bfloat16)],
        compiler_params=pltpu.CompilerParams(vmem_limit_bytes=6 * 2**20),
        cost_estimate=pl.CostEstimate(
            flops=2 * count * rows * columns * (ff + total),
            bytes_accessed=2 * count * ff * columns,
            transcendentals=0,
        ),
        name="finish",
    )(*hidden, resident(weights), slots, *others)


def activate_kernel(*refs):
    *sums, scale, out = refs
    both = sums[0][...]
    for part in sums[1:]:
        both = both + part[...].astype(jnp.float32)
    ff = out.shape[1]
    out[...] = (jax.nn.silu(both[:, :ff]) * both[:, ff:] * scale[:, :1]).astype(out.dtype)


def activate(base, arrived, scale):
    rows, wide = base.shape
    return pl.pallas_call(
        activate_kernel,
        out_shape=jax.ShapeDtypeStruct((rows, wide // 2), jnp.bfloat16),
        in_specs=in_vmem(2 + len(arrived)),
        out_specs=pl.BlockSpec(memory_space=pltpu.VMEM),
        compiler_params=pltpu.CompilerParams(vmem_limit_bytes=4 * 2**20),
        name="activate",
    )(base, *arrived, scale)


def spread(own, group):
    gathered = {0: own, 1: swap(own, "dp", 1)}
    for j in range(2, group, 2):
        gathered[j] = swap(own, "dp", j)
    return gathered


def complete(gathered, group):
    for j in range(2, group, 2):
        gathered[j + 1] = swap(gathered[j], "dp", 1)
    return [gathered[k] for k in range(group)]


def shards(tokens, expert_ids, combine_weights, w_gate, w_up, w_down):
    tok_rows, depth = tokens.shape
    top = expert_ids.shape[1]
    local_experts = w_gate.shape[0]
    ff = w_gate.shape[2]
    owners = lax.axis_size("expert")
    group = lax.axis_size("dp")
    rows = owners * CAP
    chunks = local_experts // group
    member = lax.axis_index("dp")
    first = lax.axis_index("expert") * local_experts
    places = [
        jnp.stack([member, first + c * group, jnp.int32(c * group)]) for c in range(chunks)
    ]

    order = visiting(group)
    own = pack(tokens, expert_ids, combine_weights)
    far_blocks = {far: swap(own, "expert", far) for far in range(NEAR, owners, NEAR)}
    near_blocks = {near: swap(own, "expert", near) for near in range(1, NEAR)}
    pair = (w_gate, w_up)
    (gate_ready,), token = load((w_gate,), (0,), (order[:-1],), places[0], own)
    far_blocks, token = lax.optimization_barrier((far_blocks, token))
    blocks = {0: own} | near_blocks | far_blocks
    for far in far_blocks:
        for near in range(1, NEAR):
            blocks[far + near] = swap(blocks[far], "expert", near)
    ordered = [blocks[k] for k in range(owners)]
    (up_ready,), token = load((w_up,), (0,), (order[:-1],), places[0], token)
    weights = [gate_ready, up_ready]

    hidden, slots = [], []
    natural = list(range(group))
    after = token
    sends, keeps, scales = [], [], []
    for c in range(chunks):
        ahead = 1 if c + 1 < chunks else 0
        outs = project(
            ordered, places[c], weights, pair, c * group, order, ahead, after, top, group, rows
        )
        send, *kept, scale, one_hot = outs[: 3 + group // 2]
        weights = outs[3 + group // 2 :]
        sends.append(send)
        keeps.append(kept)
        scales.append(scale)
        slots.append(one_hot)
        after = scale
    received = [swap(send, "dp", 1) for send in sends]
    bases, arrived = [], []
    for c in range(chunks):
        parts, base = merge(received[c], keeps[c])
        bases.append(base)
        arrived.append([swap(part, "dp", 2 * j) for j, part in enumerate(parts, 1)])
    after = parts[0] if parts else base
    natural = list(range(group))
    down_weights, tokens = [], []
    for c in range(chunks):
        loaded, token = load((w_down,), (c * group,), (natural,), places[0], after)
        arrived[c], hidden, token = lax.optimization_barrier((arrived[c], hidden, token))
        after = activate(bases[c], arrived[c], scales[c])
        hidden.append(spread(after, group))
        down_weights += loaded
        tokens.append(token)
    last = hidden.pop()
    hidden = [complete(gathered, group) for gathered in hidden]
    others = [down(hidden[c], down_weights[c], slots[c], tokens) for c in range(chunks - 1)]
    if others:
        last, others = lax.optimization_barrier((last, others))
    hidden.append(complete(last, group))
    columns = depth // COLUMN_PARTS
    fars = range(NEAR, owners, NEAR)
    nears = range(1, NEAR)
    partials = [
        finish(hidden[-1], down_weights[-1], slots[-1], others, start, columns, owners)
        for start in range(0, depth, columns)
    ]
    passing = [
        {far: [swap(partial[far + near], "expert", near) for near in nears] for far in fars}
        for partial in partials
    ]
    own_parts, _ = lax.optimization_barrier(
        ([partial[:NEAR] for partial in partials], partials[-1][NEAR:])
    )
    done = []
    for partial, mine, received in zip(partials, own_parts, passing):
        total = mine[0]
        for near in nears:
            total = total + swap(mine[near], "expert", near).astype(jnp.float32)
        for far in fars:
            part = partial[far]
            for block in received[far]:
                part = part + block.astype(jnp.float32)
            part = swap(part.astype(jnp.bfloat16), "expert", far)
            total = total + part.astype(jnp.float32)
        done.append(total.astype(jnp.bfloat16))
    return jnp.concatenate(done, axis=1)


def fits(owners, group, tokens, expert_ids, w_gate):
    powers = all(k & (k - 1) == 0 for k in (owners, group))
    return (
        powers
        and owners >= NEAR
        and group >= 2
        and w_gate.shape[0] % group == 0
        and tokens.shape[0] % 16 == 0
        and (owners * CAP) % 16 == 0
        and owners * CAP < 256
        and owners * w_gate.shape[0] <= 256
        and 4 * expert_ids.shape[1] <= LANES
        and tokens.shape[1] % (COLUMN_PARTS * LANES) == 0
        and tokens.shape[1] % (16 * PIECES) == 0
        and w_gate.shape[2] % LANES == 0
        and w_gate.shape[2] % (16 * PIECES) == 0
    )


def layer(tokens, expert_ids, combine_weights, w_gate, w_up, w_down):
    owners, group = lax.axis_size("expert"), lax.axis_size("dp")
    chosen = shards if fits(owners, group, tokens, expert_ids, w_gate) else plain_shards
    return chosen(tokens, expert_ids, combine_weights, w_gate, w_up, w_down)


def solution(mesh):
    placed = (
        P("expert", "dp"),
        P("expert", None),
        P("expert", None),
        P("expert", "dp", None),
        P("expert", "dp", None),
        P("expert", None, "dp"),
    )
    return jax.shard_map(
        layer, mesh=mesh, in_specs=placed, out_specs=P("expert", "dp"), check_vma=False
    )
```

```python
import functools
import math

import jax
import jax.numpy as jnp
from jax import lax
from jax.experimental import pallas as pl
from jax.experimental.pallas import tpu as pltpu
from jax.sharding import PartitionSpec as P

CAP = 10
NEAR = 4
LANES = 128
PIECES = 4
BASE_VMEM = 5 * 2**20
COLUMN_PARTS = 2


def plain_shards(tokens, expert_ids, combine_weights, w_gate, w_up, w_down):
    tok_rows, width_part = tokens.shape
    top_count = expert_ids.shape[1]
    local_experts = w_gate.shape[0]
    owners = lax.axis_size("expert")
    experts = local_experts * owners
    expert_iota = lax.broadcasted_iota(jnp.int32, (1, 1, experts), 2)
    matches = (expert_ids[:, :, None] == expert_iota).astype(jnp.int32)
    per_token = jnp.sum(matches, axis=1)
    before = jnp.cumsum(per_token, axis=0) - per_token
    position = jnp.sum(matches * before[:, None, :], axis=2)
    slot_index = expert_ids * CAP + position
    slot_iota = lax.broadcasted_iota(jnp.int32, (experts * CAP, 1, 1), 0)
    placed = jnp.any(slot_index[None, :, :] == slot_iota, axis=2).astype(jnp.bfloat16)
    outgoing = jnp.dot(placed, tokens, preferred_element_type=jnp.float32).astype(jnp.bfloat16)
    incoming = lax.all_to_all(outgoing, "expert", split_axis=0, concat_axis=0, tiled=True)
    arrived = incoming.reshape(owners, local_experts, CAP, width_part)
    gate_part = jnp.einsum("hecd,edf->hecf", arrived, w_gate, preferred_element_type=jnp.float32)
    up_part = jnp.einsum("hecd,edf->hecf", arrived, w_up, preferred_element_type=jnp.float32)
    gate_sum, up_sum = (
        lax.psum_scatter(gate_part, "dp", scatter_dimension=0, tiled=True),
        lax.psum_scatter(up_part, "dp", scatter_dimension=0, tiled=True),
    )
    shares = (jax.nn.silu(gate_sum) * up_sum).astype(jnp.bfloat16)
    hidden = lax.all_gather(shares, "dp", axis=0, tiled=True)
    outputs = jnp.einsum(
        "hecf,efd->hecd", hidden, w_down, preferred_element_type=jnp.float32
    ).astype(jnp.bfloat16)
    returned = lax.all_to_all(
        outputs.reshape(owners * local_experts * CAP, width_part),
        "expert",
        split_axis=0,
        concat_axis=0,
        tiled=True,
    )
    picked = jnp.take(returned, slot_index.reshape(-1), axis=0).reshape(
        tok_rows, top_count, width_part
    )
    combined = jnp.sum(combine_weights[:, :, None] * picked.astype(jnp.float32), axis=1)
    return combined.astype(jnp.bfloat16)


def swap(value, axis, distance):
    size = lax.axis_size(axis)
    return lax.ppermute(value, axis, [(i, i ^ distance) for i in range(size)])


def resident(value):
    return pltpu.with_memory_space_constraint(value, pltpu.VMEM)


def distant(value):
    return pltpu.with_memory_space_constraint(value, pltpu.HBM)


def in_vmem(count):
    return [pl.BlockSpec(memory_space=pltpu.VMEM)] * count


def anywhere(count):
    return [pl.BlockSpec(memory_space=pl.ANY)] * count


def in_hbm(count):
    return [pl.BlockSpec(memory_space=pltpu.HBM)] * count


def pack_kernel(tokens, ids, weights, packed):
    depth = tokens.shape[1]
    weight = weights[...]
    high = weight.astype(jnp.bfloat16).astype(jnp.float32)
    middle = (weight - high).astype(jnp.bfloat16).astype(jnp.float32)
    low = weight - high - middle
    rows = jnp.concatenate((ids[...].astype(jnp.float32), high, middle, low), axis=0)
    count = rows.shape[0]
    row = lax.broadcasted_iota(jnp.int32, (count, LANES), 0)
    col = lax.broadcasted_iota(jnp.int32, (count, LANES), 1)
    eye = jnp.where(row == col, 1.0, 0.0).astype(jnp.bfloat16)
    packed[:, :depth] = tokens[...]
    packed[:, depth:] = lax.dot_general(
        rows.astype(jnp.bfloat16),
        eye,
        (((0,), (0,)), ((), ())),
        preferred_element_type=jnp.float32,
    ).astype(jnp.bfloat16)


def pack(tokens, expert_ids, combine_weights):
    rows, depth = tokens.shape
    return pl.pallas_call(
        pack_kernel,
        out_shape=jax.ShapeDtypeStruct((rows, depth + LANES), jnp.bfloat16),
        in_specs=in_vmem(3),
        out_specs=pl.BlockSpec(memory_space=pltpu.VMEM),
        name="pack",
    )(tokens, expert_ids.T, combine_weights.T)


def total_kernel(parts, *refs):
    out = refs[-1]
    count = (len(refs) - 1) // parts
    columns = out.shape[1] // parts
    for p in range(parts):
        first, *others = refs[p * count : (p + 1) * count]
        total = first[...]
        for other in others:
            total = total + other[...].astype(jnp.float32)
        out[:, p * columns : (p + 1) * columns] = total.astype(out.dtype)


def add_up(terms):
    rows, columns = terms[0][0].shape
    flat = [term for part in terms for term in part]
    return pl.pallas_call(
        functools.partial(total_kernel, len(terms)),
        out_shape=jax.ShapeDtypeStruct((rows, columns * len(terms)), jnp.bfloat16),
        in_specs=in_vmem(len(flat)),
        out_specs=pl.BlockSpec(memory_space=pltpu.VMEM),
        compiler_params=pltpu.CompilerParams(vmem_limit_bytes=8 * 2**20),
        name="add_up",
    )(*flat)


def visiting(group):
    return list(range(1, group, 2)) + list(range(0, group, 2))[::-1]


def load_kernel(starts, orders, place, *refs):
    count = len(starts)
    sources, targets = refs[:count], refs[count + 1 : 2 * count + 1]
    token, done = refs[-2:]
    copies = []
    for k in range(max(map(len, orders))):
        for i in range(count):
            if k < len(orders[i]):
                expert = starts[i] + (orders[i][k] ^ place[0])
                rows = targets[i].shape[1] // PIECES
                for j in range(PIECES):
                    copies.append(
                        pltpu.make_async_copy(
                            sources[i].at[expert, pl.ds(j * rows, rows)],
                            targets[i].at[k, pl.ds(j * rows, rows)],
                            done.at[i, k, j],
                        )
                    )
                    copies[-1].start()
    token[...] = jnp.zeros_like(token)
    for copy in copies:
        copy.wait()


def load(weights, starts, orders, place, after):
    count = len(weights)
    shapes = [
        pltpu.VMEM((len(order),) + w.shape[1:], w.dtype) for w, order in zip(weights, orders)
    ]
    size = sum(2 * math.prod(shape.shape) for shape in shapes)
    *loaded, token = pl.pallas_call(
        functools.partial(load_kernel, starts, orders),
        out_shape=shapes + [jax.ShapeDtypeStruct((8, LANES), jnp.float32)],
        in_specs=[pl.BlockSpec(memory_space=pltpu.SMEM)] + in_hbm(count) + anywhere(1),
        out_specs=in_vmem(count + 1),
        scratch_shapes=[pltpu.SemaphoreType.DMA((count, max(map(len, orders)), PIECES))],
        compiler_params=pltpu.CompilerParams(vmem_limit_bytes=2 * 2**20),
        cost_estimate=pl.CostEstimate(flops=0, bytes_accessed=size, transcendentals=0),
        name="load",
    )(place, *map(distant, weights), after)
    return loaded, token


def merge_kernel(half, *refs):
    received, keeps, parts, base = refs[0], refs[1 : 1 + half], refs[1 + half : -1], refs[-1]
    base[...] = keeps[0][...] + received[0].astype(jnp.float32)
    for j, part in enumerate(parts):
        part[...] = (keeps[j + 1][...] + received[j + 1].astype(jnp.float32)).astype(part.dtype)


def merge(received, keeps):
    half = len(keeps)
    shape = keeps[0].shape
    *parts, base = pl.pallas_call(
        functools.partial(merge_kernel, half),
        out_shape=[jax.ShapeDtypeStruct(shape, jnp.bfloat16)] * (half - 1)
        + [jax.ShapeDtypeStruct(shape, jnp.float32)],
        in_specs=in_vmem(1 + half),
        out_specs=in_vmem(half),
        compiler_params=pltpu.CompilerParams(vmem_limit_bytes=4 * 2**20),
        name="merge",
    )(received, *keeps)
    return parts, base


def route(blocks, held, picked, scale, slots, place, top, group, rows):
    depth = held.shape[1] - LANES
    tok_rows = blocks[0].shape[0]
    total = held.shape[0]
    member, first = place[0], place[1]
    for k, block in enumerate(blocks):
        held[k * tok_rows : (k + 1) * tok_rows, :] = block[...]
    meta = held[:, depth:].astype(jnp.float32)
    lane = lax.broadcasted_iota(jnp.int32, (1, LANES), 1)
    named = jnp.where(lane < group, first + (lane ^ member), -1).astype(jnp.float32)
    match = jnp.zeros((total, LANES), jnp.float32)
    for k in range(top):
        match = match + jnp.where(meta[:, k : k + 1] == named, 1.0, 0.0)
    row = lax.broadcasted_iota(jnp.int32, (total, total), 0)
    col = lax.broadcasted_iota(jnp.int32, (total, total), 1)
    earlier = jnp.where(row > col, 1.0, 0.0).astype(jnp.bfloat16)
    position = jnp.dot(earlier, match.astype(jnp.bfloat16), preferred_element_type=jnp.float32)
    position = jnp.where(match > 0.0, position, -1.0).astype(jnp.bfloat16)
    width = group * rows
    wide_row = lax.broadcasted_iota(jnp.int32, (LANES, width), 0)
    wide_col = lax.broadcasted_iota(jnp.int32, (LANES, width), 1)
    inside = (wide_col >= wide_row * rows) & (wide_col < (wide_row + 1) * rows)
    spread = jnp.where(inside, 1.0, 0.0).astype(jnp.bfloat16)
    wide = jnp.dot(position, spread, preferred_element_type=jnp.float32)
    number = lax.broadcasted_iota(jnp.int32, (1, width), 1)
    slot = number
    for j in range(1, group):
        slot = slot - jnp.where(number >= j * rows, rows, 0)
    one_hot = jnp.where(wide == slot.astype(jnp.float32), 1.0, 0.0).astype(jnp.bfloat16)
    slots[...] = one_hot
    step = 3 * LANES
    for begin in range(0, held.shape[1], step):
        end = min(begin + step, held.shape[1])
        picked[:, begin:end] = lax.dot_general(
            one_hot,
            held[:, begin:end],
            (((0,), (0,)), ((), ())),
            preferred_element_type=jnp.float32,
        ).astype(jnp.bfloat16)
    own = picked[:rows, depth:].astype(jnp.float32)
    weight = (own[:, top : 2 * top] + own[:, 2 * top : 3 * top]) + own[:, 3 * top : 4 * top]
    mine = (first + member).astype(jnp.float32)
    weight = jnp.sum(jnp.where(own[:, :top] == mine, weight, 0.0), axis=1, keepdims=True)
    scale[...] = jnp.broadcast_to(weight, scale.shape)


def project_kernel(top, group, rows, numbers, owners, stream, ahead, place, *refs):
    refs = list(refs)

    def take(count):
        taken, refs[:count] = refs[:count], []
        return taken

    blocks, weights = take(owners), take(2)
    near = weights[0].shape[0]
    streamed = len(numbers) - near
    far = take(2) if streamed or ahead else []
    take(1)
    half = group // 2
    send, keeps = take(1)[0], take(half)
    scale, slots = take(2)
    targets = take(2) if ahead else []
    held, picked = take(2)
    copies = {}
    if streamed:
        buffers, arrivals = take(2), take(1)[0]
        for k in range(streamed):
            for i in range(2):
                copies[i, k] = pltpu.make_async_copy(
                    far[i].at[stream + (numbers[near + k] ^ place[0])],
                    buffers[i].at[k],
                    arrivals.at[i, k],
                )
                copies[i, k].start()
    waiting = []
    if ahead:
        fetched = take(1)[0]
        for i in range(2):
            for k in range(ahead):
                waiting.append(
                    pltpu.make_async_copy(
                        far[i].at[stream + group + (numbers[k] ^ place[0])],
                        targets[i].at[k],
                        fetched.at[i, k],
                    )
                )
                waiting[-1].start()
    depth, ff = weights[0].shape[1:]

    @pl.when(place[0] >= 0)
    def _():
        route(blocks, held, picked, scale, slots, place, top, group, rows)
        for k, number in enumerate(numbers):
            for i in range(2):
                if k >= near:
                    copies[i, k - near].wait()
                part = jnp.dot(
                    picked[number * rows : (number + 1) * rows, :depth],
                    weights[i][k] if k < near else buffers[i][k - near],
                    preferred_element_type=jnp.float32,
                )
                if number % 2:
                    send[number // 2, :, i * ff : (i + 1) * ff] = part.astype(send.dtype)
                else:
                    keeps[number // 2][:, i * ff : (i + 1) * ff] = part

    for copy in waiting:
        copy.wait()


def project(blocks, place, weights, pair, stream, numbers, ahead, after, top, group, rows):
    depth, ff = weights[0].shape[1:]
    owners = len(blocks)
    tok_rows, wide = blocks[0].shape
    total = tok_rows * owners
    half = group // 2
    streamed = len(numbers) - weights[0].shape[0]
    pair = list(pair) if streamed or ahead else []
    out_shape = [jax.ShapeDtypeStruct((half, rows, 2 * ff), jnp.bfloat16)]
    out_shape += [jax.ShapeDtypeStruct((rows, 2 * ff), jnp.float32)] * half
    out_shape += [
        jax.ShapeDtypeStruct((rows, LANES), jnp.float32),
        jax.ShapeDtypeStruct((total, group * rows), jnp.bfloat16),
    ]
    out_shape += [pltpu.VMEM((ahead, depth, ff), jnp.bfloat16)] * (2 * (ahead > 0))
    scratch = [
        pltpu.VMEM((total, wide), jnp.bfloat16),
        pltpu.VMEM((group * rows, wide), jnp.bfloat16),
    ]
    if streamed:
        scratch += [pltpu.VMEM((streamed, depth, ff), jnp.bfloat16)] * 2
        scratch += [pltpu.SemaphoreType.DMA((2, streamed))]
    if ahead:
        scratch += [pltpu.SemaphoreType.DMA((2, ahead))]
    return pl.pallas_call(
        functools.partial(project_kernel, top, group, rows, numbers, owners, stream, ahead),
        out_shape=out_shape,
        in_specs=[pl.BlockSpec(memory_space=pltpu.SMEM)]
        + in_vmem(owners + 2)
        + in_hbm(len(pair))
        + anywhere(1),
        out_specs=in_vmem(len(out_shape)),
        scratch_shapes=scratch,
        compiler_params=pltpu.CompilerParams(
            vmem_limit_bytes=BASE_VMEM + streamed * depth * ff * 4
        ),
        cost_estimate=pl.CostEstimate(
            flops=4 * len(numbers) * rows * depth * ff,
            bytes_accessed=4 * len(numbers) * depth * ff,
            transcendentals=0,
        ),
        name="project",
    )(place, *blocks, *map(resident, weights), *map(distant, pair), after)


def down_kernel(count, *refs):
    hidden, weights, slots = refs[:count], refs[count], refs[count + 1]
    total, result = refs[-2:]
    rows = hidden[0].shape[0]
    for k, part in enumerate(hidden):
        result[k * rows : (k + 1) * rows, :] = jnp.dot(
            part[...], weights[k], preferred_element_type=jnp.float32
        ).astype(jnp.bfloat16)
    total[...] = jnp.dot(slots[...], result[...], preferred_element_type=jnp.float32)


def down(hidden, weights, slots, after):
    rows, ff = hidden[0].shape
    count, columns = len(hidden), weights.shape[2]
    total = slots.shape[0]
    return pl.pallas_call(
        functools.partial(down_kernel, count),
        out_shape=jax.ShapeDtypeStruct((total, columns), jnp.float32),
        in_specs=in_vmem(count + 2) + anywhere(len(after)),
        out_specs=pl.BlockSpec(memory_space=pltpu.VMEM),
        scratch_shapes=[pltpu.VMEM((count * rows, columns), jnp.bfloat16)],
        compiler_params=pltpu.CompilerParams(vmem_limit_bytes=6 * 2**20),
        cost_estimate=pl.CostEstimate(
            flops=2 * count * rows * columns * (ff + total),
            bytes_accessed=2 * count * ff * columns,
            transcendentals=0,
        ),
        name="down",
    )(*hidden, resident(weights), slots, *after)


def finish_kernel(count, chunks, start, columns, *refs):
    hidden, weights, slots = refs[:count], refs[count], refs[count + 1]
    others = refs[count + 2 : count + 1 + chunks]
    outs, result = refs[count + 1 + chunks : -1], refs[-1]
    rows = hidden[0].shape[0]
    for k, part in enumerate(hidden):
        result[k * rows : (k + 1) * rows, :] = jnp.dot(
            part[...],
            weights[k, :, start : start + columns],
            preferred_element_type=jnp.float32,
        ).astype(jnp.bfloat16)
    total = jnp.dot(slots[...], result[...], preferred_element_type=jnp.float32)
    for other in others:
        total = total + other[:, start : start + columns]
    tok_rows = outs[0].shape[0]
    for k, out in enumerate(outs):
        out[...] = total[k * tok_rows : (k + 1) * tok_rows, :].astype(out.dtype)


def finish(hidden, weights, slots, others, start, columns, owners):
    rows, ff = hidden[0].shape
    count = len(hidden)
    total = slots.shape[0]
    out_shape = [
        jax.ShapeDtypeStruct(
            (total // owners, columns), jnp.float32 if k % NEAR == 0 else jnp.bfloat16
        )
        for k in range(owners)
    ]
    return pl.pallas_call(
        functools.partial(finish_kernel, count, len(others) + 1, start, columns),
        out_shape=out_shape,
        in_specs=in_vmem(count + 2 + len(others)),
        out_specs=in_vmem(owners),
        scratch_shapes=[pltpu.VMEM((count * rows, columns), jnp.bfloat16)],
        compiler_params=pltpu.CompilerParams(vmem_limit_bytes=6 * 2**20),
        cost_estimate=pl.CostEstimate(
            flops=2 * count * rows * columns * (ff + total),
            bytes_accessed=2 * count * ff * columns,
            transcendentals=0,
        ),
        name="finish",
    )(*hidden, resident(weights), slots, *others)


def activate_kernel(*refs):
    *sums, scale, out = refs
    both = sums[0][...]
    for part in sums[1:]:
        both = both + part[...].astype(jnp.float32)
    ff = out.shape[1]
    out[...] = (jax.nn.silu(both[:, :ff]) * both[:, ff:] * scale[:, :1]).astype(out.dtype)


def activate(base, arrived, scale):
    rows, wide = base.shape
    return pl.pallas_call(
        activate_kernel,
        out_shape=jax.ShapeDtypeStruct((rows, wide // 2), jnp.bfloat16),
        in_specs=in_vmem(2 + len(arrived)),
        out_specs=pl.BlockSpec(memory_space=pltpu.VMEM),
        compiler_params=pltpu.CompilerParams(vmem_limit_bytes=4 * 2**20),
        name="activate",
    )(base, *arrived, scale)


def spread(own, group):
    gathered = {0: own, 1: swap(own, "dp", 1)}
    for j in range(2, group, 2):
        gathered[j] = swap(own, "dp", j)
    return gathered


def complete(gathered, group):
    for j in range(2, group, 2):
        gathered[j + 1] = swap(gathered[j], "dp", 1)
    return [gathered[k] for k in range(group)]


def shards(tokens, expert_ids, combine_weights, w_gate, w_up, w_down):
    tok_rows, depth = tokens.shape
    top = expert_ids.shape[1]
    local_experts = w_gate.shape[0]
    ff = w_gate.shape[2]
    owners = lax.axis_size("expert")
    group = lax.axis_size("dp")
    rows = owners * CAP
    chunks = local_experts // group
    member = lax.axis_index("dp")
    first = lax.axis_index("expert") * local_experts
    places = [
        jnp.stack([member, first + c * group, jnp.int32(c * group)]) for c in range(chunks)
    ]

    order = visiting(group)
    own = pack(tokens, expert_ids, combine_weights)
    far_blocks = {far: swap(own, "expert", far) for far in range(NEAR, owners, NEAR)}
    near_blocks = {near: swap(own, "expert", near) for near in range(1, NEAR)}
    pair = (w_gate, w_up)
    (gate_ready,), token = load((w_gate,), (0,), (order[:-1],), places[0], own)
    far_blocks, token = lax.optimization_barrier((far_blocks, token))
    blocks = {0: own} | near_blocks | far_blocks
    for far in far_blocks:
        for near in range(1, NEAR):
            blocks[far + near] = swap(blocks[far], "expert", near)
    ordered = [blocks[k] for k in range(owners)]
    (up_ready,), token = load((w_up,), (0,), (order[:-1],), places[0], token)
    weights = [gate_ready, up_ready]

    hidden, slots = [], []
    natural = list(range(group))
    after = token
    sends, keeps, scales = [], [], []
    for c in range(chunks):
        ahead = 1 if c + 1 < chunks else 0
        outs = project(
            ordered, places[c], weights, pair, c * group, order, ahead, after, top, group, rows
        )
        send, *kept, scale, one_hot = outs[: 3 + group // 2]
        weights = outs[3 + group // 2 :]
        sends.append(send)
        keeps.append(kept)
        scales.append(scale)
        slots.append(one_hot)
        after = scale
    received = [swap(send, "dp", 1) for send in sends]
    bases, arrived = [], []
    for c in range(chunks):
        parts, base = merge(received[c], keeps[c])
        bases.append(base)
        arrived.append([swap(part, "dp", 2 * j) for j, part in enumerate(parts, 1)])
    after = parts[0] if parts else base
    natural = list(range(group))
    down_weights, tokens = [], []
    for c in range(chunks):
        loaded, token = load((w_down,), (c * group,), (natural,), places[0], after)
        arrived[c], hidden, token = lax.optimization_barrier((arrived[c], hidden, token))
        after = activate(bases[c], arrived[c], scales[c])
        hidden.append(spread(after, group))
        down_weights += loaded
        tokens.append(token)
    last = hidden.pop()
    hidden = [complete(gathered, group) for gathered in hidden]
    others = [down(hidden[c], down_weights[c], slots[c], tokens) for c in range(chunks - 1)]
    if others:
        last, others = lax.optimization_barrier((last, others))
    hidden.append(complete(last, group))
    columns = depth // COLUMN_PARTS
    fars = range(NEAR, owners, NEAR)
    nears = range(1, NEAR)
    partials = [
        finish(hidden[-1], down_weights[-1], slots[-1], others, start, columns, owners)
        for start in range(0, depth, columns)
    ]
    passing = [
        {far: [swap(partial[far + near], "expert", near) for near in nears] for far in fars}
        for partial in partials
    ]
    own_parts, _ = lax.optimization_barrier(
        ([partial[:NEAR] for partial in partials], partials[-1][NEAR:])
    )
    done = []
    for partial, mine, received in zip(partials, own_parts, passing):
        terms = [mine[0]] + [swap(mine[near], "expert", near) for near in nears]
        for far in fars:
            part = partial[far]
            for block in received[far]:
                part = part + block.astype(jnp.float32)
            terms.append(swap(part.astype(jnp.bfloat16), "expert", far))
        done.append(terms)
    return add_up(done)


def fits(owners, group, tokens, expert_ids, w_gate):
    powers = all(k & (k - 1) == 0 for k in (owners, group))
    return (
        powers
        and owners >= NEAR
        and group >= 2
        and w_gate.shape[0] % group == 0
        and tokens.shape[0] % 16 == 0
        and (owners * CAP) % 16 == 0
        and owners * CAP < 256
        and owners * w_gate.shape[0] <= 256
        and 4 * expert_ids.shape[1] <= LANES
        and tokens.shape[1] % (COLUMN_PARTS * LANES) == 0
        and tokens.shape[1] % (16 * PIECES) == 0
        and w_gate.shape[2] % LANES == 0
        and w_gate.shape[2] % (16 * PIECES) == 0
    )


def layer(tokens, expert_ids, combine_weights, w_gate, w_up, w_down):
    owners, group = lax.axis_size("expert"), lax.axis_size("dp")
    chosen = shards if fits(owners, group, tokens, expert_ids, w_gate) else plain_shards
    return chosen(tokens, expert_ids, combine_weights, w_gate, w_up, w_down)


def solution(mesh):
    placed = (
        P("expert", "dp"),
        P("expert", None),
        P("expert", None),
        P("expert", "dp", None),
        P("expert", "dp", None),
        P("expert", None, "dp"),
    )
    return jax.shard_map(
        layer, mesh=mesh, in_specs=placed, out_specs=P("expert", "dp"), check_vma=False
    )
```
